32 devices in a mesh: lat: 8 (over z, y), wave: 4 (over x, core).
Axes of the slice: x: 2, y: 2, z: 4, core: 2. Of those that a mesh axis runs over, the one named last changes fastest.
Arguments:
- fourier: bfloat16 [1280, 1280, 128], P(('lat', 'wave')), may hold values from -6 to 6
- legendre: bfloat16 [640, 1281, 640], P(('lat', 'wave')), may hold values from -0.25 to 0.25
- pair_table: int32 [640], replicated, may hold values from 0 to 639, each once
- row_lat: int32 [1280], replicated, may hold values from 0 to 1279, each once
- gauss_weight: float32 [640], replicated, may hold values from 0.3 to 3
- layer_pressure_matrix: float32 [16, 16], replicated, may hold values from -1.5 to 1.5
- modes: float32 [16, 16], replicated, may hold values from -1.5 to 1.5
- mode_depth: float32 [16], replicated, may hold values from 0.1 to 10
- diffusion: float32 [4, 16], replicated, may hold values from 0.1 to 4
Outputs:
- fourier_out: bfloat16 [1280, 1280, 128], P(('lat', 'wave'))
- spectrum: float32 [1280, 64], P(('lat', 'wave'))
The draws below stay inside these ranges and needn't reach their ends.
Inputs may be any that keep to these rules, and one draw needn't show every extreme that they name: pair_table is a permutation of 0..639. row_lat is a permutation of 0..1279.
All inputs are finite; a program needn't handle non-finite values.
Results may differ from the reference program's by a relative error of at most 0.0055.
Values may be sent and summed in bfloat16 or wider, within the bound.
No kernel may reach another device: no remote copies, remote signals or barrier semaphores. Data moves between devices by JAX's collectives and lax.ppermute only.
A program may use at most 320 MiB of HBM per device.

```python
import math
import jax
import jax.numpy as jnp
from jax import lax

TRUNC = 1279
NLAT = 1280
FIELDS = 4
LEVELS = 16
WAVES = 1280
NPAIR = 640
NPACK = 1281
NHALF = 640
COLS = 128


def levels(rng, shape, cuts, least, top_value):
    factor_of = 1.0
    for axis_at, blocks in cuts:
        steps = jax.random.uniform(jax.random.fold_in(jax.random.fold_in(rng, 6), axis_at), (blocks,), jnp.float32, least / len(cuts), top_value / len(cuts))
        factor_of = factor_of * jnp.repeat(jnp.exp(steps), shape[axis_at] // blocks).reshape((-1,) + (1,) * (len(shape) - 1 - axis_at))
    return factor_of


def noise(key, extent, deviation, bound, cuts=(), kind=jnp.bfloat16):
    array = deviation * jax.random.normal(key, extent, jnp.float32)
    if cuts:
        array = array * levels(key, extent, cuts, -0.22, 0.18)
    return jnp.clip(array, -bound, bound).astype(kind)


def setup_inputs(seed: int = 0) -> dict:
    arg_keys = jax.random.split(jax.random.key(seed), 10)
    fourier = noise(arg_keys[0], (NLAT, WAVES, COLS), 1.0, 6.0, ((0, 32),))
    legendre = noise(arg_keys[1], (NPAIR, NPACK, NHALF), NHALF ** -0.5, 0.25, ((0, 32),))
    pair_table = jax.random.permutation(arg_keys[2], NPAIR).astype(jnp.int32)
    row_lat = jax.random.permutation(arg_keys[3], NLAT).astype(jnp.int32)
    gauss_weight = jnp.clip(jnp.exp(jax.random.uniform(arg_keys[4], (NHALF,), jnp.float32, math.log(0.3), math.log(3.0))), 0.3, 3.0)
    layer_pressure_matrix = noise(arg_keys[5], (LEVELS, LEVELS), LEVELS ** -0.5, 1.5, (), jnp.float32)
    modes = noise(arg_keys[6], (LEVELS, LEVELS), LEVELS ** -0.5, 1.5, (), jnp.float32)
    mode_depth = jnp.clip(jnp.exp(jax.random.uniform(arg_keys[7], (LEVELS,), jnp.float32, math.log(0.1), math.log(10.0))), 0.1, 10.0)
    diffusion = jnp.clip(jnp.exp(jax.random.uniform(arg_keys[8], (FIELDS, LEVELS), jnp.float32, math.log(0.1), math.log(4.0))), 0.1, 4.0)
    return dict(fourier=fourier, legendre=legendre, pair_table=pair_table, row_lat=row_lat, gauss_weight=gauss_weight, layer_pressure_matrix=layer_pressure_matrix, modes=modes, mode_depth=mode_depth, diffusion=diffusion)


def place_energy(energy, order):
    degrees = jnp.arange(WAVES, dtype=jnp.int32)
    padded = jnp.concatenate([jnp.zeros((WAVES, FIELDS * LEVELS), energy.dtype), energy], axis=0)
    lower = lax.dynamic_slice_in_dim(padded, (WAVES - order).astype(jnp.int32), WAVES, 0)
    upper = jnp.where((degrees >= TRUNC - order)[:, None], energy[1:], jnp.zeros_like(energy[1:]))
    return lower + upper


def pair_step(legendre_slab, folded, order, layer_pressure_matrix, modes, mode_depth, diffusion):
    packed = jnp.arange(NPACK, dtype=jnp.int32)
    in_first = packed <= TRUNC - order
    odd_first = packed % 2 == 1
    odd_second = (packed + order + TRUNC + 1) % 2 == 1
    degree = jnp.where(in_first, order + packed, packed - 1)
    gathered = jnp.dot(legendre_slab, folded, preferred_element_type=jnp.float32).reshape(NPACK, 4, COLS)
    spectral = jnp.where(in_first[:, None], jnp.where(odd_first[:, None], gathered[:, 1], gathered[:, 0]),
                         jnp.where(odd_second[:, None], gathered[:, 3], gathered[:, 2]))
    evolving_state_arrays = spectral.reshape(NPACK, 2, FIELDS, LEVELS)
    scale = (degree * (degree + 1)).astype(jnp.float32) / jnp.float32(TRUNC * (TRUNC + 1))
    backward_step_weight = scale[:, None, None]
    rotation_rate_coeffs = evolving_state_arrays[:, :, 0]
    velocity_spread_coeffs = evolving_state_arrays[:, :, 1]
    thermal_state_coeffs = evolving_state_arrays[:, :, 2]
    moisture_mass_ratio = evolving_state_arrays[:, :, 3]
    maximal_harmonic_index = lax.Precision.HIGHEST
    source_tendency = velocity_spread_coeffs + backward_step_weight * jnp.matmul(thermal_state_coeffs, layer_pressure_matrix, precision=maximal_harmonic_index)
    modal_part = jnp.matmul(source_tendency, modes, precision=maximal_harmonic_index) / (1.0 + backward_step_weight * mode_depth)
    advanced_velocity_spread = jnp.matmul(modal_part, modes.T, precision=maximal_harmonic_index)
    advanced_thermal_state = thermal_state_coeffs - jnp.matmul(advanced_velocity_spread, layer_pressure_matrix.T, precision=maximal_harmonic_index)
    advanced_state_arrays = jnp.stack([rotation_rate_coeffs, advanced_velocity_spread, advanced_thermal_state, moisture_mass_ratio], axis=2)
    advanced_state_arrays = advanced_state_arrays / (1.0 + diffusion * (scale * scale)[:, None, None, None])
    weight = jnp.where(in_first & (order == 0), 1.0, 2.0).astype(advanced_state_arrays.dtype)
    energy = weight[:, None] * (advanced_state_arrays[:, 0] * advanced_state_arrays[:, 0] + advanced_state_arrays[:, 1] * advanced_state_arrays[:, 1]).reshape(NPACK, FIELDS * LEVELS)
    placed = place_energy(energy, order)
    rounded = advanced_state_arrays.reshape(NPACK, COLS).astype(jnp.bfloat16)
    nothing = jnp.zeros_like(rounded)
    blocks = jnp.stack([jnp.where((in_first & ~odd_first)[:, None], rounded, nothing),
                        jnp.where((in_first & odd_first)[:, None], rounded, nothing),
                        jnp.where((~in_first & ~odd_second)[:, None], rounded, nothing),
                        jnp.where((~in_first & odd_second)[:, None], rounded, nothing)], axis=1).reshape(NPACK, 4 * COLS)
    synthesis = lax.dot_general(legendre_slab, blocks, (((0,), (0,)), ((), ())),
                                preferred_element_type=jnp.float32).reshape(NHALF, 2, 2, COLS)
    northern = (synthesis[:, :, 0] + synthesis[:, :, 1]).astype(jnp.bfloat16)
    southern = (synthesis[:, :, 0] - synthesis[:, :, 1]).astype(jnp.bfloat16)
    rebuilt = jnp.concatenate([northern, southern[::-1]], axis=0)
    return placed, rebuilt


def reference(fourier, legendre, pair_table, row_lat, gauss_weight, layer_pressure_matrix, modes, mode_depth, diffusion):
    positions = jnp.arange(NLAT, dtype=jnp.int32)
    row_place = jnp.zeros((NLAT,), jnp.int32).at[row_lat].set(positions)
    latitudes = jnp.take(fourier, row_place, axis=0)
    northern = latitudes[:NHALF]
    southern = latitudes[::-1][:NHALF]

    def one_pair(spectrum, inputs):
        legendre_slab, order = inputs
        picks = jnp.stack([order, TRUNC - order]).astype(jnp.int32)
        north_cols = jnp.take(northern, picks, axis=1).astype(jnp.float32)
        south_cols = jnp.take(southern, picks, axis=1).astype(jnp.float32)
        symmetric = north_cols + south_cols
        antisym = north_cols - south_cols
        folded = (gauss_weight[:, None, None, None] * jnp.stack([symmetric, antisym], axis=2)).astype(jnp.bfloat16)
        folded = folded.reshape(NHALF, 4 * COLS)
        placed, rebuilt = pair_step(legendre_slab, folded, order, layer_pressure_matrix, modes, mode_depth, diffusion)
        return spectrum + placed, rebuilt

    spectrum, rebuilt = lax.scan(one_pair, jnp.zeros((WAVES, FIELDS * LEVELS), jnp.float32), (legendre, pair_table))
    slot_wave = jnp.stack([pair_table, TRUNC - pair_table], axis=1).reshape(WAVES).astype(jnp.int32)
    slot_of_wave = jnp.zeros((WAVES,), jnp.int32).at[slot_wave].set(jnp.arange(WAVES, dtype=jnp.int32))
    by_slot = jnp.transpose(rebuilt, (1, 0, 2, 3)).reshape(NLAT, WAVES, COLS)
    natural = jnp.take(by_slot, slot_of_wave, axis=1)
    fourier_out = jnp.take(natural, row_lat, axis=0)
    return fourier_out, spectrum
```

```python
import jax
import jax.numpy as jnp
from jax import lax
from jax.experimental import pallas as pl
from jax.experimental.pallas import tpu as pltpu
from jax.sharding import PartitionSpec as P

TRUNC = 1279
NLAT = 1280
FIELDS = 4
LEVELS = 16
WAVES = 1280
NPACK = 1281
NHALF = 640
COLS = 128
PITCH = 1288
KTILE = 256
NTAIL = 16
AXES = ("lat", "wave")
VMEM = 60 << 20
BF16 = jnp.bfloat16
F32 = jnp.float32


def divisor_up_to(number, most):
    return max(d for d in range(1, most + 1) if number % d == 0)


def gather_waves(pair_table, fourier, devices, local_pairs, first, count, padded):
    rows = fourier.shape[0]
    per_read = divisor_up_to(rows, 8)
    reads = rows // per_read
    per_write = divisor_up_to(devices, 4)

    def body(table, rows_ref, out_ref, held):
        step = pl.program_id(0)

        if padded > rows:

            @pl.when(step == 0)
            def _():
                held[rows * PITCH :, :] = jnp.zeros(((padded - rows) * PITCH, COLS), F32)

        @pl.when(step < reads)
        def _():
            for r in range(per_read):
                start = pl.multiple_of((step * per_read + r) * PITCH, 8)
                held[pl.ds(start, WAVES), :] = rows_ref[r].astype(F32)

        @pl.when(step >= reads)
        def _():
            def one_device(d, carry):
                for s in range(count):
                    wave = table[((step - reads) * per_write + d) * local_pairs + first + s]
                    both = jnp.concatenate(
                        [
                            held[pl.ds(wave, padded, stride=PITCH), :],
                            held[pl.ds(TRUNC - wave, padded, stride=PITCH), :],
                        ],
                        axis=0,
                    )
                    out_ref[d, pl.ds(s * 2 * padded, 2 * padded), :] = both.astype(BF16)
                return carry

            lax.fori_loop(0, per_write, one_device, 0)

    return pl.pallas_call(
        body,
        grid_spec=pltpu.PrefetchScalarGridSpec(
            num_scalar_prefetch=1,
            grid=(reads + devices // per_write,),
            in_specs=[
                pl.BlockSpec((per_read, WAVES, COLS), lambda i, t: (jnp.minimum(i, reads - 1), 0, 0))
            ],
            out_specs=pl.BlockSpec(
                (per_write, count * 2 * padded, COLS), lambda i, t: (jnp.maximum(i - reads, 0), 0, 0)
            ),
            scratch_shapes=[pltpu.VMEM((padded * PITCH, COLS), F32)],
        ),
        out_shape=jax.ShapeDtypeStruct((devices, count * 2 * padded, COLS), BF16),
        compiler_params=pltpu.CompilerParams(vmem_limit_bytes=VMEM),
        cost_estimate=pl.CostEstimate(flops=0, bytes_accessed=20_000_000, transcendentals=0),
        name="gather_waves",
    )(pair_table, fourier)


def scatter_waves(pair_table, chunks, spans, rows, devices, local_pairs, padded):
    per_read = divisor_up_to(devices, 4)
    reads = devices // per_read
    per_write = divisor_up_to(rows, 8)
    writes = rows // per_write

    def body(table, *refs):
        chunk_refs, out_ref, held = refs[: len(chunks)], refs[-2], refs[-1]
        step = pl.program_id(0)

        @pl.when(step < reads)
        def _():
            for (first, count), chunk_ref in zip(spans, chunk_refs):

                def one_device(d, carry, first=first, count=count, chunk_ref=chunk_ref):
                    for s in range(count):
                        wave = table[(step * per_read + d) * local_pairs + first + s]
                        both = chunk_ref[d, pl.ds(s * 2 * padded, 2 * padded), :].astype(F32)
                        held[pl.ds(wave, padded, stride=PITCH), :] = both[:padded]
                        held[pl.ds(TRUNC - wave, padded, stride=PITCH), :] = both[padded:]
                    return carry

                lax.fori_loop(0, per_read, one_device, 0)

        @pl.when(step >= reads)
        def _():
            for r in range(per_write):
                start = pl.multiple_of(((step - reads) * per_write + r) * PITCH, 8)
                out_ref[r] = held[pl.ds(start, WAVES), :].astype(BF16)

    return pl.pallas_call(
        body,
        grid_spec=pltpu.PrefetchScalarGridSpec(
            num_scalar_prefetch=1,
            grid=(reads + writes,),
            in_specs=[
                pl.BlockSpec(
                    (per_read, count * 2 * padded, COLS), lambda i, t: (jnp.minimum(i, reads - 1), 0, 0)
                )
                for _, count in spans
            ],
            out_specs=pl.BlockSpec(
                (per_write, WAVES, COLS), lambda i, t: (jnp.maximum(i - reads, 0), 0, 0)
            ),
            scratch_shapes=[pltpu.VMEM((padded * PITCH, COLS), F32)],
        ),
        out_shape=jax.ShapeDtypeStruct((rows, WAVES, COLS), BF16),
        compiler_params=pltpu.CompilerParams(vmem_limit_bytes=VMEM),
        cost_estimate=pl.CostEstimate(flops=0, bytes_accessed=26_000_000, transcendentals=0),
        name="scatter_waves",
    )(pair_table, *chunks)


def transform(orders, arrived, legendre, fold, unfold, weight, first_map, second_map, depth, damping, first, count, padded):
    devices = arrived.shape[0]
    all_rows = devices * padded

    def body(
        orders_ref, arrived_ref, legendre_ref, fold_ref, unfold_ref, weight_ref, map1_ref, map2_ref, depth_ref,
        damping_ref, out_ref, low_ref, high_ref, rows_in, folded, blocks, halves, tail,
    ):
        step = pl.program_id(0)
        order = orders_ref[first + step]

        @pl.when(step == 0)
        def _():
            low_ref[...] = jnp.zeros_like(low_ref)
            high_ref[...] = jnp.zeros_like(high_ref)
            tail[...] = jnp.zeros_like(tail)

        tail[0:1, :] = legendre_ref[0, NPACK - 1 : NPACK, :]

        arrived_rows = arrived_ref[...].astype(F32)
        rows_in[:, :COLS] = arrived_rows[:, :padded].reshape(all_rows, COLS).astype(BF16)
        rows_in[:, COLS:] = arrived_rows[:, padded:].reshape(all_rows, COLS).astype(BF16)

        def fold_tile(i, carry):
            at = pl.multiple_of(i * 128, 128)
            for part in range(2):
                sums = jnp.dot(
                    fold_ref[pl.ds(pl.multiple_of(part * NHALF + at, 128), 128), :],
                    rows_in[...],
                    preferred_element_type=F32,
                )
                folded[pl.ds(at, 128), part * 256 : part * 256 + 256] = (
                    weight_ref[pl.ds(at, 128), :] * sums
                ).astype(BF16)
            return carry

        lax.fori_loop(0, NHALF // 128, fold_tile, 0)

        def update(start, slab, size):
            gathered = jnp.dot(slab, folded[...], preferred_element_type=F32)
            packed = lax.broadcasted_iota(jnp.int32, (size, COLS), 0) + start
            in_first = packed <= TRUNC - order
            odd = jnp.where(in_first, packed, packed + order) % 2 == 1
            spectral = jnp.where(
                in_first,
                jnp.where(odd, gathered[:, 2 * COLS : 3 * COLS], gathered[:, :COLS]),
                jnp.where(odd, gathered[:, 3 * COLS :], gathered[:, COLS : 2 * COLS]),
            )
            degree = jnp.where(in_first, order + packed, packed - 1)
            scale = (degree * (degree + 1)).astype(F32) / F32(TRUNC * (TRUNC + 1))
            forced = jnp.dot(
                spectral, map1_ref[...], precision=lax.Precision.HIGHEST, preferred_element_type=F32
            )
            modal = (forced[:, :COLS] + scale * forced[:, COLS:]) / (1.0 + scale * depth_ref[...])
            evolved = jnp.dot(
                modal, map2_ref[...], precision=lax.Precision.HIGHEST, preferred_element_type=F32
            )
            field = (lax.broadcasted_iota(jnp.int32, (size, COLS), 1) // LEVELS) % FIELDS
            updated = (jnp.where(field == 1, 0.0, spectral) + evolved) / (
                1.0 + damping_ref[...] * (scale * scale)
            )
            energy = jnp.where(in_first & (order == 0), 1.0, 2.0) * (updated * updated)
            nothing = jnp.zeros_like(updated)
            for block, chosen in enumerate(
                (in_first & ~odd, ~in_first & ~odd, in_first & odd, ~in_first & odd)
            ):
                blocks[pl.ds(start, size), block * COLS : (block + 1) * COLS] = jnp.where(
                    chosen, updated, nothing
                ).astype(BF16)
            low = jnp.where(in_first, energy, nothing)
            high_ref[pl.ds(start, size), :] += energy - low
            return low

        def update_tile(i, carry):
            start = pl.multiple_of(i * KTILE, KTILE)
            low = update(start, legendre_ref[0, pl.ds(start, KTILE), :], KTILE)
            low_ref[pl.ds(start + order, KTILE), :] += low
            return carry

        lax.fori_loop(0, (NPACK - 1) // KTILE, update_tile, 0)
        update(NPACK - 1, tail[...], NTAIL)

        def synthesis_tile(i, carry):
            at = pl.multiple_of(i * 128, 128)
            both = lax.dot_general(
                legendre_ref[0, : NPACK - 1, pl.ds(at, 128)],
                blocks[: NPACK - 1, :],
                (((0,), (0,)), ((), ())),
                preferred_element_type=F32,
            ) + lax.dot_general(
                tail[:, pl.ds(at, 128)],
                blocks[NPACK - 1 :, :],
                (((0,), (0,)), ((), ())),
                preferred_element_type=F32,
            )
            halves[pl.ds(at, 128), :] = (both[:, :256] + both[:, 256:]).astype(BF16)
            halves[pl.ds(pl.multiple_of(NHALF + at, 128), 128), :] = (
                both[:, :256] - both[:, 256:]
            ).astype(BF16)
            return carry

        lax.fori_loop(0, NHALF // 128, synthesis_tile, 0)

        back = jnp.dot(unfold_ref[...], halves[...], preferred_element_type=F32)
        out_ref[...] = jnp.concatenate(
            [
                back[:, :COLS].reshape(devices, padded, COLS),
                back[:, COLS:].reshape(devices, padded, COLS),
            ],
            axis=1,
        ).astype(BF16)

    whole = lambda shape: pl.BlockSpec(shape, lambda i, t: (0,) * len(shape))
    return pl.pallas_call(
        body,
        grid_spec=pltpu.PrefetchScalarGridSpec(
            num_scalar_prefetch=1,
            grid=(count,),
            in_specs=[
                pl.BlockSpec((devices, 2 * padded, COLS), lambda i, t: (0, i, 0)),
                pl.BlockSpec((1, NPACK, NHALF), lambda i, t: (first + i, 0, 0)),
                whole(fold.shape),
                whole(unfold.shape),
                whole(weight.shape),
                whole(first_map.shape),
                whole(second_map.shape),
                whole(depth.shape),
                whole(damping.shape),
            ],
            out_specs=[
                pl.BlockSpec((devices, 2 * padded, COLS), lambda i, t: (0, i, 0)),
                whole((2 * WAVES, COLS)),
                whole((WAVES + NTAIL, COLS)),
            ],
            scratch_shapes=[
                pltpu.VMEM((all_rows, 2 * COLS), BF16),
                pltpu.VMEM((NHALF, 4 * COLS), BF16),
                pltpu.VMEM((WAVES + NTAIL, 4 * COLS), BF16),
                pltpu.VMEM((NLAT, 2 * COLS), BF16),
                pltpu.VMEM((NTAIL, NHALF), BF16),
            ],
        ),
        out_shape=[
            jax.ShapeDtypeStruct(arrived.shape, BF16),
            jax.ShapeDtypeStruct((2 * WAVES, COLS), F32),
            jax.ShapeDtypeStruct((WAVES + NTAIL, COLS), F32),
        ],
        compiler_params=pltpu.CompilerParams(vmem_limit_bytes=VMEM),
        cost_estimate=pl.CostEstimate(
            flops=count * 3_500_000_000, bytes_accessed=count * 3_000_000, transcendentals=0
        ),
        name="transform",
    )(orders, arrived, legendre, fold, unfold, weight, first_map, second_map, depth, damping)


def field_map(parts):
    one = jnp.zeros((FIELDS, LEVELS, FIELDS, LEVELS), F32)
    for source, target, matrix in parts:
        one = one.at[source, :, target, :].set(matrix)
    one = one.reshape(COLS // 2, COLS // 2)
    nothing = jnp.zeros_like(one)
    return jnp.concatenate(
        [jnp.concatenate([one, nothing], axis=1), jnp.concatenate([nothing, one], axis=1)], axis=0
    )


def on_device(
    fourier, legendre, pair_table, row_lat, gauss_weight, layer_pressure_matrix, modes, mode_depth, diffusion
):
    devices = lax.axis_size("lat") * lax.axis_size("wave")
    rows = fourier.shape[0]
    local_pairs = legendre.shape[0]
    padded = -(-rows // 8) * 8
    chunks = min(2, local_pairs)
    cuts = [local_pairs * c // chunks for c in range(chunks + 1)]
    spans = [(cuts[c], cuts[c + 1] - cuts[c]) for c in range(chunks)]
    own = lax.dynamic_slice_in_dim(
        pair_table, lax.axis_index(AXES) * local_pairs, local_pairs
    )

    lat = jnp.pad(
        row_lat.reshape(devices, rows), ((0, 0), (0, padded - rows)), constant_values=-1
    ).reshape(-1)
    half = jnp.arange(NHALF, dtype=jnp.int32)
    north_rows = (lat[None, :] == half[:, None]).astype(BF16)
    south_rows = (lat[None, :] == NLAT - 1 - half[:, None]).astype(BF16)
    fold = jnp.concatenate([north_rows + south_rows, north_rows - south_rows], axis=0)
    unfold = jnp.concatenate(
        [lat[:, None] == half[None, :], lat[:, None] == NLAT - 1 - half[None, :]], axis=1
    ).astype(BF16)
    high = lax.Precision.HIGHEST
    first_map = jnp.concatenate(
        [
            field_map([(1, 1, modes)]),
            field_map([(2, 1, jnp.dot(layer_pressure_matrix, modes, precision=high))]),
        ],
        axis=1,
    )
    second_map = field_map(
        [
            (1, 1, modes.T),
            (1, 2, -jnp.dot(modes.T, layer_pressure_matrix.T, precision=high)),
        ]
    )
    depth = jnp.tile(
        jnp.zeros((FIELDS, LEVELS), F32).at[1].set(mode_depth).reshape(1, -1), (1, 2)
    )
    damping = jnp.tile(diffusion.reshape(1, -1), (1, 2))

    outgoing = [
        gather_waves(pair_table, fourier, devices, local_pairs, first, count, padded)
        for first, count in spans
    ]
    arrived = [lax.all_to_all(block, AXES, 0, 0, tiled=True) for block in outgoing]
    done = [
        transform(
            own, block, legendre, fold, unfold, gauss_weight.reshape(NHALF, 1), first_map, second_map,
            depth, damping, first, count, padded,
        )
        for block, (first, count) in zip(arrived, spans)
    ]
    energy = sum(low[:WAVES] + high[1 : WAVES + 1] for _, low, high in done)
    spectrum = lax.psum_scatter(
        energy[:, : COLS // 2] + energy[:, COLS // 2 :], AXES, scatter_dimension=0, tiled=True
    )
    back = [lax.all_to_all(block, AXES, 0, 0, tiled=True) for block, _, _ in done]
    fourier_out = scatter_waves(pair_table, back, spans, rows, devices, local_pairs, padded)
    return (fourier_out, spectrum)


def solution(mesh):
    split = P(AXES, None, None)
    placed = (split, split, P(), P(), P(), P(), P(), P(), P())
    return jax.shard_map(
        on_device,
        mesh=mesh,
        in_specs=placed,
        out_specs=(split, P(AXES, None)),
        check_vma=False,
    )
```

```python
import jax
import jax.numpy as jnp
from jax import lax
from jax.experimental import pallas as pl
from jax.experimental.pallas import tpu as pltpu
from jax.sharding import PartitionSpec as P

TRUNC = 1279
NLAT = 1280
FIELDS = 4
LEVELS = 16
WAVES = 1280
NPACK = 1281
NHALF = 640
COLS = 128
PITCH = 1288
KTILE = 256
NTAIL = 16
AXES = ("lat", "wave")
VMEM = 60 << 20
BF16 = jnp.bfloat16
F32 = jnp.float32


def divisor_up_to(number, most):
    return max(d for d in range(1, most + 1) if number % d == 0)


def gather_waves(pair_table, fourier, devices, local_pairs, first, count, padded):
    rows = fourier.shape[0]
    per_read = divisor_up_to(rows, 8)
    reads = rows // per_read
    per_write = divisor_up_to(devices, 4)

    def body(table, rows_ref, out_ref, held):
        step = pl.program_id(0)

        if padded > rows:

            @pl.when(step == 0)
            def _():
                held[rows * PITCH :, :] = jnp.zeros(((padded - rows) * PITCH, COLS), F32)

        @pl.when(step < reads)
        def _():
            for r in range(per_read):
                start = pl.multiple_of((step * per_read + r) * PITCH, 8)
                held[pl.ds(start, WAVES), :] = rows_ref[r].astype(F32)

        @pl.when(step >= reads)
        def _():
            def one_device(d, carry):
                for s in range(count):
                    wave = table[((step - reads) * per_write + d) * local_pairs + first + s]
                    both = jnp.concatenate(
                        [
                            held[pl.ds(wave, padded, stride=PITCH), :],
                            held[pl.ds(TRUNC - wave, padded, stride=PITCH), :],
                        ],
                        axis=0,
                    )
                    out_ref[d, pl.ds(s * 2 * padded, 2 * padded), :] = both.astype(BF16)
                return carry

            lax.fori_loop(0, per_write, one_device, 0)

    return pl.pallas_call(
        body,
        grid_spec=pltpu.PrefetchScalarGridSpec(
            num_scalar_prefetch=1,
            grid=(reads + devices // per_write,),
            in_specs=[
                pl.BlockSpec((per_read, WAVES, COLS), lambda i, t: (jnp.minimum(i, reads - 1), 0, 0))
            ],
            out_specs=pl.BlockSpec(
                (per_write, count * 2 * padded, COLS), lambda i, t: (jnp.maximum(i - reads, 0), 0, 0)
            ),
            scratch_shapes=[pltpu.VMEM((padded * PITCH, COLS), F32)],
        ),
        out_shape=jax.ShapeDtypeStruct((devices, count * 2 * padded, COLS), BF16),
        compiler_params=pltpu.CompilerParams(vmem_limit_bytes=VMEM),
        cost_estimate=pl.CostEstimate(flops=0, bytes_accessed=20_000_000, transcendentals=0),
        name="gather_waves",
    )(pair_table, fourier)


def scatter_waves(pair_table, chunks, spans, rows, devices, local_pairs, padded):
    per_read = divisor_up_to(devices, 4)
    reads = devices // per_read
    per_write = divisor_up_to(rows, 8)
    writes = rows // per_write

    def body(table, *refs):
        chunk_refs, out_ref, held = refs[: len(chunks)], refs[-2], refs[-1]
        step = pl.program_id(0)

        @pl.when(step < reads)
        def _():
            for (first, count), chunk_ref in zip(spans, chunk_refs):

                def one_device(d, carry, first=first, count=count, chunk_ref=chunk_ref):
                    for s in range(count):
                        wave = table[(step * per_read + d) * local_pairs + first + s]
                        both = chunk_ref[d, pl.ds(s * 2 * padded, 2 * padded), :].astype(F32)
                        held[pl.ds(wave, padded, stride=PITCH), :] = both[:padded]
                        held[pl.ds(TRUNC - wave, padded, stride=PITCH), :] = both[padded:]
                    return carry

                lax.fori_loop(0, per_read, one_device, 0)

        @pl.when(step >= reads)
        def _():
            for r in range(per_write):
                start = pl.multiple_of(((step - reads) * per_write + r) * PITCH, 8)
                out_ref[r] = held[pl.ds(start, WAVES), :].astype(BF16)

    return pl.pallas_call(
        body,
        grid_spec=pltpu.PrefetchScalarGridSpec(
            num_scalar_prefetch=1,
            grid=(reads + writes,),
            in_specs=[
                pl.BlockSpec(
                    (per_read, count * 2 * padded, COLS), lambda i, t: (jnp.minimum(i, reads - 1), 0, 0)
                )
                for _, count in spans
            ],
            out_specs=pl.BlockSpec(
                (per_write, WAVES, COLS), lambda i, t: (jnp.maximum(i - reads, 0), 0, 0)
            ),
            scratch_shapes=[pltpu.VMEM((padded * PITCH, COLS), F32)],
        ),
        out_shape=jax.ShapeDtypeStruct((rows, WAVES, COLS), BF16),
        compiler_params=pltpu.CompilerParams(vmem_limit_bytes=VMEM),
        cost_estimate=pl.CostEstimate(flops=0, bytes_accessed=26_000_000, transcendentals=0),
        name="scatter_waves",
    )(pair_table, *chunks)


def transform(orders, arrived, legendre, fold, unfold, weight, first_map, second_map, depth, damping, first, count, padded):
    devices = arrived.shape[0]
    all_rows = devices * padded

    def body(
        orders_ref, arrived_ref, legendre_ref, fold_ref, unfold_ref, weight_ref, map1_ref, map2_ref, depth_ref,
        damping_ref, out_ref, low_ref, high_ref, rows_in, folded, blocks, halves, tail,
    ):
        step = pl.program_id(0)
        order = orders_ref[first + step]

        @pl.when(step == 0)
        def _():
            low_ref[...] = jnp.zeros_like(low_ref)
            high_ref[...] = jnp.zeros_like(high_ref)
            tail[...] = jnp.zeros_like(tail)

        tail[0:1, :] = legendre_ref[0, NPACK - 1 : NPACK, :]

        arrived_rows = arrived_ref[...].astype(F32)
        rows_in[:, :COLS] = arrived_rows[:, :padded].reshape(all_rows, COLS).astype(BF16)
        rows_in[:, COLS:] = arrived_rows[:, padded:].reshape(all_rows, COLS).astype(BF16)

        def fold_tile(i, carry):
            at = pl.multiple_of(i * 128, 128)
            for part in range(2):
                sums = jnp.dot(
                    fold_ref[pl.ds(pl.multiple_of(part * NHALF + at, 128), 128), :],
                    rows_in[...],
                    preferred_element_type=F32,
                )
                folded[pl.ds(at, 128), part * 256 : part * 256 + 256] = (
                    weight_ref[pl.ds(at, 128), :] * sums
                ).astype(BF16)
            return carry

        lax.fori_loop(0, NHALF // 128, fold_tile, 0)

        def update(start, slab, size):
            gathered = jnp.dot(slab, folded[...], preferred_element_type=F32)
            packed = lax.broadcasted_iota(jnp.int32, (size, COLS), 0) + start
            in_first = packed <= TRUNC - order
            odd = jnp.where(in_first, packed, packed + order) % 2 == 1
            spectral = jnp.where(
                in_first,
                jnp.where(odd, gathered[:, 2 * COLS : 3 * COLS], gathered[:, :COLS]),
                jnp.where(odd, gathered[:, 3 * COLS :], gathered[:, COLS : 2 * COLS]),
            )
            degree = jnp.where(in_first, order + packed, packed - 1)
            scale = (degree * (degree + 1)).astype(F32) / F32(TRUNC * (TRUNC + 1))
            forced = jnp.dot(
                spectral, map1_ref[...], precision=lax.Precision.HIGHEST, preferred_element_type=F32
            )
            modal = (forced[:, :COLS] + scale * forced[:, COLS:]) / (1.0 + scale * depth_ref[...])
            evolved = jnp.dot(
                modal, map2_ref[...], precision=lax.Precision.HIGHEST, preferred_element_type=F32
            )
            field = (lax.broadcasted_iota(jnp.int32, (size, COLS), 1) // LEVELS) % FIELDS
            updated = (jnp.where(field == 1, 0.0, spectral) + evolved) / (
                1.0 + damping_ref[...] * (scale * scale)
            )
            energy = jnp.where(in_first & (order == 0), 1.0, 2.0) * (updated * updated)
            nothing = jnp.zeros_like(updated)
            for block, chosen in enumerate(
                (in_first & ~odd, ~in_first & ~odd, in_first & odd, ~in_first & odd)
            ):
                blocks[pl.ds(start, size), block * COLS : (block + 1) * COLS] = jnp.where(
                    chosen, updated, nothing
                ).astype(BF16)
            low = jnp.where(in_first, energy, nothing)
            high_ref[pl.ds(start, size), :] += energy - low
            return low

        def update_tile(i, carry):
            start = pl.multiple_of(i * KTILE, KTILE)
            low = update(start, legendre_ref[0, pl.ds(start, KTILE), :], KTILE)
            low_ref[pl.ds(start + order, KTILE), :] += low
            return carry

        lax.fori_loop(0, (NPACK - 1) // KTILE, update_tile, 0)
        update(NPACK - 1, tail[...], NTAIL)

        def synthesis_tile(i, carry):
            at = pl.multiple_of(i * 128, 128)
            both = lax.dot_general(
                legendre_ref[0, : NPACK - 1, pl.ds(at, 128)],
                blocks[: NPACK - 1, :],
                (((0,), (0,)), ((), ())),
                preferred_element_type=F32,
            ) + lax.dot_general(
                tail[:, pl.ds(at, 128)],
                blocks[NPACK - 1 :, :],
                (((0,), (0,)), ((), ())),
                preferred_element_type=F32,
            )
            halves[pl.ds(at, 128), :] = (both[:, :256] + both[:, 256:]).astype(BF16)
            halves[pl.ds(pl.multiple_of(NHALF + at, 128), 128), :] = (
                both[:, :256] - both[:, 256:]
            ).astype(BF16)
            return carry

        lax.fori_loop(0, NHALF // 128, synthesis_tile, 0)

        back = jnp.dot(unfold_ref[...], halves[...], preferred_element_type=F32)
        out_ref[...] = jnp.concatenate(
            [
                back[:, :COLS].reshape(devices, padded, COLS),
                back[:, COLS:].reshape(devices, padded, COLS),
            ],
            axis=1,
        ).astype(BF16)

    whole = lambda shape: pl.BlockSpec(shape, lambda i, t: (0,) * len(shape))
    return pl.pallas_call(
        body,
        grid_spec=pltpu.PrefetchScalarGridSpec(
            num_scalar_prefetch=1,
            grid=(count,),
            in_specs=[
                pl.BlockSpec((devices, 2 * padded, COLS), lambda i, t: (0, i, 0)),
                pl.BlockSpec((1, NPACK, NHALF), lambda i, t: (first + i, 0, 0)),
                whole(fold.shape),
                whole(unfold.shape),
                whole(weight.shape),
                whole(first_map.shape),
                whole(second_map.shape),
                whole(depth.shape),
                whole(damping.shape),
            ],
            out_specs=[
                pl.BlockSpec((devices, 2 * padded, COLS), lambda i, t: (0, i, 0)),
                whole((2 * WAVES, COLS)),
                whole((WAVES + NTAIL, COLS)),
            ],
            scratch_shapes=[
                pltpu.VMEM((all_rows, 2 * COLS), BF16),
                pltpu.VMEM((NHALF, 4 * COLS), BF16),
                pltpu.VMEM((WAVES + NTAIL, 4 * COLS), BF16),
                pltpu.VMEM((NLAT, 2 * COLS), BF16),
                pltpu.VMEM((NTAIL, NHALF), BF16),
            ],
        ),
        out_shape=[
            jax.ShapeDtypeStruct(arrived.shape, BF16),
            jax.ShapeDtypeStruct((2 * WAVES, COLS), F32),
            jax.ShapeDtypeStruct((WAVES + NTAIL, COLS), F32),
        ],
        compiler_params=pltpu.CompilerParams(vmem_limit_bytes=VMEM),
        cost_estimate=pl.CostEstimate(
            flops=count * 3_500_000_000, bytes_accessed=count * 3_000_000, transcendentals=0
        ),
        name="transform",
    )(orders, arrived, legendre, fold, unfold, weight, first_map, second_map, depth, damping)


def field_map(parts):
    one = jnp.zeros((FIELDS, LEVELS, FIELDS, LEVELS), F32)
    for source, target, matrix in parts:
        one = one.at[source, :, target, :].set(matrix)
    one = one.reshape(COLS // 2, COLS // 2)
    nothing = jnp.zeros_like(one)
    return jnp.concatenate(
        [jnp.concatenate([one, nothing], axis=1), jnp.concatenate([nothing, one], axis=1)], axis=0
    )


def scatter_sum(parts, devices):
    device = lax.axis_index(AXES)
    rows, columns = parts.shape[0] // devices, parts.shape[1]
    sums = parts.reshape(devices, rows * columns // COLS, COLS)
    bit = 1
    while bit < devices:
        sums = sums.reshape((sums.shape[0] // 2, 2) + sums.shape[1:])
        own = (device // bit) % 2
        kept = lax.dynamic_index_in_dim(sums, own, 1, keepdims=False)
        sent = lax.dynamic_index_in_dim(sums, 1 - own, 1, keepdims=False)
        sums = kept + lax.ppermute(sent, AXES, [(d, d ^ bit) for d in range(devices)])
        bit *= 2
    return sums.reshape(rows, columns)


def on_device(
    fourier, legendre, pair_table, row_lat, gauss_weight, layer_pressure_matrix, modes, mode_depth, diffusion
):
    devices = lax.axis_size("lat") * lax.axis_size("wave")
    rows = fourier.shape[0]
    local_pairs = legendre.shape[0]
    padded = -(-rows // 8) * 8
    chunks = min(2, local_pairs)
    cuts = [local_pairs * c // chunks for c in range(chunks + 1)]
    spans = [(cuts[c], cuts[c + 1] - cuts[c]) for c in range(chunks)]
    own = lax.dynamic_slice_in_dim(
        pair_table, lax.axis_index(AXES) * local_pairs, local_pairs
    )

    lat = jnp.pad(
        row_lat.reshape(devices, rows), ((0, 0), (0, padded - rows)), constant_values=-1
    ).reshape(-1)
    half = jnp.arange(NHALF, dtype=jnp.int32)
    north_rows = (lat[None, :] == half[:, None]).astype(BF16)
    south_rows = (lat[None, :] == NLAT - 1 - half[:, None]).astype(BF16)
    fold = jnp.concatenate([north_rows + south_rows, north_rows - south_rows], axis=0)
    unfold = jnp.concatenate(
        [lat[:, None] == half[None, :], lat[:, None] == NLAT - 1 - half[None, :]], axis=1
    ).astype(BF16)
    high = lax.Precision.HIGHEST
    first_map = jnp.concatenate(
        [
            field_map([(1, 1, modes)]),
            field_map([(2, 1, jnp.dot(layer_pressure_matrix, modes, precision=high))]),
        ],
        axis=1,
    )
    second_map = field_map(
        [
            (1, 1, modes.T),
            (1, 2, -jnp.dot(modes.T, layer_pressure_matrix.T, precision=high)),
        ]
    )
    depth = jnp.tile(
        jnp.zeros((FIELDS, LEVELS), F32).at[1].set(mode_depth).reshape(1, -1), (1, 2)
    )
    damping = jnp.tile(diffusion.reshape(1, -1), (1, 2))

    outgoing = [
        gather_waves(pair_table, fourier, devices, local_pairs, first, count, padded)
        for first, count in spans
    ]
    arrived = [lax.all_to_all(block, AXES, 0, 0, tiled=True) for block in outgoing]
    done = [
        transform(
            own, block, legendre, fold, unfold, gauss_weight.reshape(NHALF, 1), first_map, second_map,
            depth, damping, first, count, padded,
        )
        for block, (first, count) in zip(arrived, spans)
    ]
    energy = sum(low[:WAVES] + high[1 : WAVES + 1] for _, low, high in done)
    spectrum = scatter_sum(energy[:, : COLS // 2] + energy[:, COLS // 2 :], devices)
    back = [lax.all_to_all(block, AXES, 0, 0, tiled=True) for block, _, _ in done]
    fourier_out = scatter_waves(pair_table, back, spans, rows, devices, local_pairs, padded)
    return (fourier_out, spectrum)


def solution(mesh):
    split = P(AXES, None, None)
    placed = (split, split, P(), P(), P(), P(), P(), P(), P())
    return jax.shard_map(
        on_device,
        mesh=mesh,
        in_specs=placed,
        out_specs=(split, P(AXES, None)),
        check_vma=False,
    )
```

```python
import jax
import jax.numpy as jnp
from jax import lax
from jax.experimental import pallas as pl
from jax.experimental.pallas import tpu as pltpu
from jax.sharding import PartitionSpec as P

TRUNC = 1279
NLAT = 1280
FIELDS = 4
LEVELS = 16
WAVES = 1280
NPACK = 1281
NHALF = 640
COLS = 128
PITCH = 1288
KTILE = 256
NTAIL = 16
AXES = ("lat", "wave")
VMEM = 60 << 20
BF16 = jnp.bfloat16
F32 = jnp.float32


def divisor_up_to(number, most):
    return max(d for d in range(1, most + 1) if number % d == 0)


def row_groups(rows):
    return [(at, min(8, rows - at)) for at in range(0, rows, 8)]


def gather_waves(pair_table, fourier, devices, local_pairs, first, count):
    rows = fourier.shape[0]
    spans = row_groups(rows)
    groups = len(spans)

    def body(table, rows_ref, out_ref, read, held, written, read_sem, write_sem):
        reads = [
            pltpu.make_async_copy(rows_ref.at[pl.ds(at, size)], read.at[pl.ds(at, size)], read_sem.at[g])
            for g, (at, size) in enumerate(spans)
        ]
        writes = [
            pltpu.make_async_copy(written.at[g], out_ref.at[:, :, g], write_sem.at[g])
            for g in range(groups)
        ]
        for copy in reads:
            copy.start()
        if rows % 8:
            read[rows:] = jnp.zeros((groups * 8 - rows, WAVES, COLS), BF16)

        for g in range(groups):
            reads[g].wait()

            def widen(r, carry, g=g):
                held[pl.ds(pl.multiple_of(r * PITCH, 8), WAVES), :] = read[g * 8 + r].astype(F32)
                return carry

            lax.fori_loop(0, 8, widen, 0)

            def one_device(d, carry, g=g):
                for s in range(count):
                    wave = table[d * local_pairs + first + s]
                    both = jnp.concatenate(
                        [
                            held[pl.ds(wave, 8, stride=PITCH), :],
                            held[pl.ds(TRUNC - wave, 8, stride=PITCH), :],
                        ],
                        axis=0,
                    )
                    written[g, d, s] = both.astype(BF16)
                return carry

            lax.fori_loop(0, devices, one_device, 0)
            writes[g].start()
        for copy in writes:
            copy.wait()

    return pl.pallas_call(
        body,
        grid_spec=pltpu.PrefetchScalarGridSpec(
            num_scalar_prefetch=1,
            grid=(1,),
            in_specs=[pl.BlockSpec(memory_space=pl.ANY)],
            out_specs=pl.BlockSpec(memory_space=pl.ANY),
            scratch_shapes=[
                pltpu.VMEM((groups * 8, WAVES, COLS), BF16),
                pltpu.VMEM((8 * PITCH, COLS), F32),
                pltpu.VMEM((groups, devices, count, 16, COLS), BF16),
                pltpu.SemaphoreType.DMA((groups,)),
                pltpu.SemaphoreType.DMA((groups,)),
            ],
        ),
        out_shape=jax.ShapeDtypeStruct((devices, count, groups, 16, COLS), BF16),
        compiler_params=pltpu.CompilerParams(vmem_limit_bytes=VMEM),
        cost_estimate=pl.CostEstimate(flops=0, bytes_accessed=20_000_000, transcendentals=0),
        name="gather_waves",
    )(pair_table, fourier)


def scatter_waves(pair_table, chunks, rows, local_pairs):
    devices = chunks[0].shape[0]
    spans = row_groups(rows)
    groups = len(spans)
    counts = [chunk.shape[1] for chunk in chunks]

    def body(table, *refs):
        chunk_refs = refs[: len(chunks)]
        out_ref = refs[len(chunks)]
        parts = refs[len(chunks) + 1 : 2 * len(chunks) + 1]
        held, written, read_sem, write_sem = refs[2 * len(chunks) + 1 :]
        reads = [
            [
                pltpu.make_async_copy(chunk.at[:, :, g], part.at[g], read_sem.at[g, c])
                for c, (chunk, part) in enumerate(zip(chunk_refs, parts))
            ]
            for g in range(groups)
        ]
        writes = [
            pltpu.make_async_copy(
                written.at[g, pl.ds(0, size)], out_ref.at[pl.ds(at, size)], write_sem.at[g]
            )
            for g, (at, size) in enumerate(spans)
        ]
        for group in reads:
            for copy in group:
                copy.start()

        for g in range(groups):
            for copy in reads[g]:
                copy.wait()

            def one_device(d, carry, g=g):
                slot = 0
                for part, count in zip(parts, counts):
                    for s in range(count):
                        wave = table[d * local_pairs + slot]
                        both = part[g, d, s].astype(F32)
                        held[pl.ds(wave, 8, stride=PITCH), :] = both[:8]
                        held[pl.ds(TRUNC - wave, 8, stride=PITCH), :] = both[8:]
                        slot += 1
                return carry

            lax.fori_loop(0, devices, one_device, 0)

            def narrow(r, carry, g=g):
                row = held[pl.ds(pl.multiple_of(r * PITCH, 8), WAVES), :]
                written[g, r] = row.astype(BF16)
                return carry

            lax.fori_loop(0, 8, narrow, 0)
            writes[g].start()
        for copy in writes:
            copy.wait()

    return pl.pallas_call(
        body,
        grid_spec=pltpu.PrefetchScalarGridSpec(
            num_scalar_prefetch=1,
            grid=(1,),
            in_specs=[pl.BlockSpec(memory_space=pl.ANY)] * len(chunks),
            out_specs=pl.BlockSpec(memory_space=pl.ANY),
            scratch_shapes=[pltpu.VMEM((groups, devices, count, 16, COLS), BF16) for count in counts]
            + [
                pltpu.VMEM((8 * PITCH, COLS), F32),
                pltpu.VMEM((groups, 8, WAVES, COLS), BF16),
                pltpu.SemaphoreType.DMA((groups, len(chunks))),
                pltpu.SemaphoreType.DMA((groups,)),
            ],
        ),
        out_shape=jax.ShapeDtypeStruct((rows, WAVES, COLS), BF16),
        compiler_params=pltpu.CompilerParams(vmem_limit_bytes=VMEM),
        cost_estimate=pl.CostEstimate(flops=0, bytes_accessed=26_000_000, transcendentals=0),
        name="scatter_waves",
    )(pair_table, *chunks)


def transform(orders, arrived, legendre, fold, unfold, weight, first_map, second_map, depth, damping, first):
    devices, count, groups = arrived.shape[:3]
    all_rows = devices * groups * 8

    def body(
        orders_ref, arrived_ref, legendre_ref, fold_ref, unfold_ref, weight_ref, map1_ref, map2_ref, depth_ref,
        damping_ref, out_ref, low_ref, high_ref, rows_in, folded, blocks, halves, tail,
    ):
        step = pl.program_id(0)
        order = orders_ref[first + step]

        @pl.when(step == 0)
        def _():
            low_ref[...] = jnp.zeros_like(low_ref)
            high_ref[...] = jnp.zeros_like(high_ref)
            tail[...] = jnp.zeros_like(tail)

        tail[0:1, :] = legendre_ref[0, NPACK - 1 : NPACK, :]

        arrived_rows = arrived_ref[...].astype(F32).reshape(devices * groups, 16, COLS)
        rows_in[:, :COLS] = arrived_rows[:, :8].reshape(all_rows, COLS).astype(BF16)
        rows_in[:, COLS:] = arrived_rows[:, 8:].reshape(all_rows, COLS).astype(BF16)

        def fold_tile(i, carry):
            at = pl.multiple_of(i * 128, 128)
            for part in range(2):
                sums = jnp.dot(
                    fold_ref[pl.ds(pl.multiple_of(part * NHALF + at, 128), 128), :],
                    rows_in[...],
                    preferred_element_type=F32,
                )
                folded[pl.ds(at, 128), part * 256 : part * 256 + 256] = (
                    weight_ref[pl.ds(at, 128), :] * sums
                ).astype(BF16)
            return carry

        lax.fori_loop(0, NHALF // 128, fold_tile, 0)

        def update(start, slab, size):
            gathered = jnp.dot(slab, folded[...], preferred_element_type=F32)
            packed = lax.broadcasted_iota(jnp.int32, (size, COLS), 0) + start
            in_first = packed <= TRUNC - order
            odd = jnp.where(in_first, packed, packed + order) % 2 == 1
            spectral = jnp.where(
                in_first,
                jnp.where(odd, gathered[:, 2 * COLS : 3 * COLS], gathered[:, :COLS]),
                jnp.where(odd, gathered[:, 3 * COLS :], gathered[:, COLS : 2 * COLS]),
            )
            degree = jnp.where(in_first, order + packed, packed - 1)
            scale = (degree * (degree + 1)).astype(F32) / F32(TRUNC * (TRUNC + 1))
            forced = jnp.dot(
                spectral, map1_ref[...], precision=lax.Precision.HIGHEST, preferred_element_type=F32
            )
            modal = (forced[:, :COLS] + scale * forced[:, COLS:]) / (1.0 + scale * depth_ref[...])
            evolved = jnp.dot(
                modal, map2_ref[...], precision=lax.Precision.HIGHEST, preferred_element_type=F32
            )
            field = (lax.broadcasted_iota(jnp.int32, (size, COLS), 1) // LEVELS) % FIELDS
            updated = (jnp.where(field == 1, 0.0, spectral) + evolved) / (
                1.0 + damping_ref[...] * (scale * scale)
            )
            energy = jnp.where(in_first & (order == 0), 1.0, 2.0) * (updated * updated)
            nothing = jnp.zeros_like(updated)
            for block, chosen in enumerate(
                (in_first & ~odd, ~in_first & ~odd, in_first & odd, ~in_first & odd)
            ):
                blocks[pl.ds(start, size), block * COLS : (block + 1) * COLS] = jnp.where(
                    chosen, updated, nothing
                ).astype(BF16)
            low = jnp.where(in_first, energy, nothing)
            high_ref[pl.ds(start, size), :] += energy - low
            return low

        def update_tile(i, carry):
            start = pl.multiple_of(i * KTILE, KTILE)
            low = update(start, legendre_ref[0, pl.ds(start, KTILE), :], KTILE)
            low_ref[pl.ds(start + order, KTILE), :] += low
            return carry

        lax.fori_loop(0, (NPACK - 1) // KTILE, update_tile, 0)
        update(NPACK - 1, tail[...], NTAIL)

        def synthesis_tile(i, carry):
            at = pl.multiple_of(i * 128, 128)
            both = lax.dot_general(
                legendre_ref[0, : NPACK - 1, pl.ds(at, 128)],
                blocks[: NPACK - 1, :],
                (((0,), (0,)), ((), ())),
                preferred_element_type=F32,
            ) + lax.dot_general(
                tail[:, pl.ds(at, 128)],
                blocks[NPACK - 1 :, :],
                (((0,), (0,)), ((), ())),
                preferred_element_type=F32,
            )
            halves[pl.ds(at, 128), :] = (both[:, :256] + both[:, 256:]).astype(BF16)
            halves[pl.ds(pl.multiple_of(NHALF + at, 128), 128), :] = (
                both[:, :256] - both[:, 256:]
            ).astype(BF16)
            return carry

        lax.fori_loop(0, NHALF // 128, synthesis_tile, 0)

        back = jnp.dot(unfold_ref[...], halves[...], preferred_element_type=F32)
        both = jnp.concatenate(
            [
                back[:, :COLS].reshape(devices * groups, 8, COLS),
                back[:, COLS:].reshape(devices * groups, 8, COLS),
            ],
            axis=1,
        )
        out_ref[...] = both.astype(BF16).reshape(devices, 1, groups, 16, COLS)

    whole = lambda shape: pl.BlockSpec(shape, lambda i, t: (0,) * len(shape))
    return pl.pallas_call(
        body,
        grid_spec=pltpu.PrefetchScalarGridSpec(
            num_scalar_prefetch=1,
            grid=(count,),
            in_specs=[
                pl.BlockSpec((devices, 1, groups, 16, COLS), lambda i, t: (0, i, 0, 0, 0)),
                pl.BlockSpec((1, NPACK, NHALF), lambda i, t: (first + i, 0, 0)),
                whole(fold.shape),
                whole(unfold.shape),
                whole(weight.shape),
                whole(first_map.shape),
                whole(second_map.shape),
                whole(depth.shape),
                whole(damping.shape),
            ],
            out_specs=[
                pl.BlockSpec((devices, 1, groups, 16, COLS), lambda i, t: (0, i, 0, 0, 0)),
                whole((2 * WAVES, COLS)),
                whole((WAVES + NTAIL, COLS)),
            ],
            scratch_shapes=[
                pltpu.VMEM((all_rows, 2 * COLS), BF16),
                pltpu.VMEM((NHALF, 4 * COLS), BF16),
                pltpu.VMEM((WAVES + NTAIL, 4 * COLS), BF16),
                pltpu.VMEM((NLAT, 2 * COLS), BF16),
                pltpu.VMEM((NTAIL, NHALF), BF16),
            ],
        ),
        out_shape=[
            jax.ShapeDtypeStruct(arrived.shape, BF16),
            jax.ShapeDtypeStruct((2 * WAVES, COLS), F32),
            jax.ShapeDtypeStruct((WAVES + NTAIL, COLS), F32),
        ],
        compiler_params=pltpu.CompilerParams(vmem_limit_bytes=VMEM),
        cost_estimate=pl.CostEstimate(
            flops=count * 3_500_000_000, bytes_accessed=count * 3_000_000, transcendentals=0
        ),
        name="transform",
    )(orders, arrived, legendre, fold, unfold, weight, first_map, second_map, depth, damping)


def field_map(parts):
    one = jnp.zeros((FIELDS, LEVELS, FIELDS, LEVELS), F32)
    for source, target, matrix in parts:
        one = one.at[source, :, target, :].set(matrix)
    one = one.reshape(COLS // 2, COLS // 2)
    nothing = jnp.zeros_like(one)
    return jnp.concatenate(
        [jnp.concatenate([one, nothing], axis=1), jnp.concatenate([nothing, one], axis=1)], axis=0
    )


def scatter_sum(parts, devices):
    device = lax.axis_index(AXES)
    rows, columns = parts.shape[0] // devices, parts.shape[1]
    sums = parts.reshape(devices, rows * columns // COLS, COLS)
    bit = 1
    while bit < devices:
        sums = sums.reshape((sums.shape[0] // 2, 2) + sums.shape[1:])
        own = (device // bit) % 2
        kept = lax.dynamic_index_in_dim(sums, own, 1, keepdims=False)
        sent = lax.dynamic_index_in_dim(sums, 1 - own, 1, keepdims=False)
        sums = kept + lax.ppermute(sent, AXES, [(d, d ^ bit) for d in range(devices)])
        bit *= 2
    return sums.reshape(rows, columns)


def exchange(block):
    flat = block.reshape(block.shape[0], -1, COLS)
    return lax.all_to_all(flat, AXES, 0, 0, tiled=True).reshape(block.shape)


def on_device(
    fourier, legendre, pair_table, row_lat, gauss_weight, layer_pressure_matrix, modes, mode_depth, diffusion
):
    devices = lax.axis_size("lat") * lax.axis_size("wave")
    rows = fourier.shape[0]
    local_pairs = legendre.shape[0]
    padded = -(-rows // 8) * 8
    chunks = min(2, local_pairs)
    cuts = [local_pairs * c // chunks for c in range(chunks + 1)]
    spans = [(cuts[c], cuts[c + 1] - cuts[c]) for c in range(chunks)]
    own = lax.dynamic_slice_in_dim(
        pair_table, lax.axis_index(AXES) * local_pairs, local_pairs
    )

    lat = jnp.pad(
        row_lat.reshape(devices, rows), ((0, 0), (0, padded - rows)), constant_values=-1
    ).reshape(-1)
    half = jnp.arange(NHALF, dtype=jnp.int32)
    north_rows = (lat[None, :] == half[:, None]).astype(BF16)
    south_rows = (lat[None, :] == NLAT - 1 - half[:, None]).astype(BF16)
    fold = jnp.concatenate([north_rows + south_rows, north_rows - south_rows], axis=0)
    unfold = jnp.concatenate(
        [lat[:, None] == half[None, :], lat[:, None] == NLAT - 1 - half[None, :]], axis=1
    ).astype(BF16)
    high = lax.Precision.HIGHEST
    first_map = jnp.concatenate(
        [
            field_map([(1, 1, modes)]),
            field_map([(2, 1, jnp.dot(layer_pressure_matrix, modes, precision=high))]),
        ],
        axis=1,
    )
    second_map = field_map(
        [
            (1, 1, modes.T),
            (1, 2, -jnp.dot(modes.T, layer_pressure_matrix.T, precision=high)),
        ]
    )
    depth = jnp.tile(
        jnp.zeros((FIELDS, LEVELS), F32).at[1].set(mode_depth).reshape(1, -1), (1, 2)
    )
    damping = jnp.tile(diffusion.reshape(1, -1), (1, 2))

    outgoing = [
        gather_waves(pair_table, fourier, devices, local_pairs, first, count)
        for first, count in spans
    ]
    arrived = [exchange(block) for block in outgoing]
    done = [
        transform(
            own, block, legendre, fold, unfold, gauss_weight.reshape(NHALF, 1), first_map, second_map,
            depth, damping, first,
        )
        for block, (first, _) in zip(arrived, spans)
    ]
    energy = sum(low[:WAVES] + high[1 : WAVES + 1] for _, low, high in done)
    spectrum = scatter_sum(energy[:, : COLS // 2] + energy[:, COLS // 2 :], devices)
    back = [exchange(block) for block, _, _ in done]
    fourier_out = scatter_waves(pair_table, back, rows, local_pairs)
    return (fourier_out, spectrum)


def solution(mesh):
    split = P(AXES, None, None)
    placed = (split, split, P(), P(), P(), P(), P(), P(), P())
    return jax.shard_map(
        on_device,
        mesh=mesh,
        in_specs=placed,
        out_specs=(split, P(AXES, None)),
        check_vma=False,
    )
```

```python
import jax
import jax.numpy as jnp
from jax import lax
from jax.experimental import pallas as pl
from jax.experimental.pallas import tpu as pltpu
from jax.sharding import PartitionSpec as P

TRUNC = 1279
NLAT = 1280
FIELDS = 4
LEVELS = 16
WAVES = 1280
NPACK = 1281
NHALF = 640
COLS = 128
PITCH = 1288
KTILE = 256
NTAIL = 16
AXES = ("lat", "wave")
VMEM = 60 << 20
BF16 = jnp.bfloat16
F32 = jnp.float32


def divisor_up_to(number, most):
    return max(d for d in range(1, most + 1) if number % d == 0)


def row_groups(rows):
    return [(at, min(8, rows - at)) for at in range(0, rows, 8)]


def gather_waves(pair_table, fourier, devices, local_pairs, first, count):
    rows = fourier.shape[0]
    spans = row_groups(rows)
    groups = len(spans)

    def body(table, rows_ref, out_ref, read, held, written, read_sem, write_sem):
        reads = [
            pltpu.make_async_copy(rows_ref.at[pl.ds(at, size)], read.at[pl.ds(at, size)], read_sem.at[g])
            for g, (at, size) in enumerate(spans)
        ]
        writes = [
            pltpu.make_async_copy(written.at[g], out_ref.at[:, :, g], write_sem.at[g])
            for g in range(groups)
        ]
        for copy in reads:
            copy.start()
        if rows % 8:
            read[rows:] = jnp.zeros((groups * 8 - rows, WAVES, COLS), BF16)

        for g in range(groups):
            reads[g].wait()

            def widen(r, carry, g=g):
                held[pl.ds(pl.multiple_of(r * PITCH, 8), WAVES), :] = read[g * 8 + r].astype(F32)
                return carry

            lax.fori_loop(0, 8, widen, 0)

            def one_device(d, carry, g=g):
                for s in range(count):
                    wave = table[d * local_pairs + first + s]
                    both = jnp.concatenate(
                        [
                            held[pl.ds(wave, 8, stride=PITCH), :],
                            held[pl.ds(TRUNC - wave, 8, stride=PITCH), :],
                        ],
                        axis=0,
                    )
                    written[g, d, s] = both.astype(BF16)
                return carry

            lax.fori_loop(0, devices, one_device, 0)
            writes[g].start()
        for copy in writes:
            copy.wait()

    return pl.pallas_call(
        body,
        grid_spec=pltpu.PrefetchScalarGridSpec(
            num_scalar_prefetch=1,
            grid=(1,),
            in_specs=[pl.BlockSpec(memory_space=pl.ANY)],
            out_specs=pl.BlockSpec(memory_space=pl.ANY),
            scratch_shapes=[
                pltpu.VMEM((groups * 8, WAVES, COLS), BF16),
                pltpu.VMEM((9 * PITCH, COLS), F32),
                pltpu.VMEM((groups, devices, count, 16, COLS), BF16),
                pltpu.SemaphoreType.DMA((groups,)),
                pltpu.SemaphoreType.DMA((groups,)),
            ],
        ),
        out_shape=jax.ShapeDtypeStruct((devices, count, groups, 16, COLS), BF16),
        compiler_params=pltpu.CompilerParams(vmem_limit_bytes=VMEM),
        cost_estimate=pl.CostEstimate(flops=0, bytes_accessed=20_000_000, transcendentals=0),
        name="gather_waves",
    )(pair_table, fourier)


def scatter_waves(pair_table, chunks, rows, local_pairs):
    devices = chunks[0].shape[0]
    spans = row_groups(rows)
    groups = len(spans)
    counts = [chunk.shape[1] for chunk in chunks]

    def body(table, *refs):
        chunk_refs = refs[: len(chunks)]
        out_ref = refs[len(chunks)]
        parts = refs[len(chunks) + 1 : 2 * len(chunks) + 1]
        held, written, read_sem, write_sem = refs[2 * len(chunks) + 1 :]
        reads = [
            [
                pltpu.make_async_copy(chunk.at[:, :, g], part.at[g], read_sem.at[g, c])
                for c, (chunk, part) in enumerate(zip(chunk_refs, parts))
            ]
            for g in range(groups)
        ]
        writes = [
            pltpu.make_async_copy(
                written.at[g, pl.ds(0, size)], out_ref.at[pl.ds(at, size)], write_sem.at[g]
            )
            for g, (at, size) in enumerate(spans)
        ]
        for group in reads:
            for copy in group:
                copy.start()

        for g in range(groups):
            for copy in reads[g]:
                copy.wait()

            def one_device(d, carry, g=g):
                slot = 0
                for part, count in zip(parts, counts):
                    for s in range(count):
                        wave = table[d * local_pairs + slot]
                        both = part[g, d, s].astype(F32)
                        held[pl.ds(wave, 8, stride=PITCH), :] = both[:8]
                        held[pl.ds(TRUNC - wave, 8, stride=PITCH), :] = both[8:]
                        slot += 1
                return carry

            lax.fori_loop(0, devices, one_device, 0)

            def narrow(r, carry, g=g):
                row = held[pl.ds(pl.multiple_of(r * PITCH, 8), WAVES), :]
                written[g, r] = row.astype(BF16)
                return carry

            lax.fori_loop(0, 8, narrow, 0)
            writes[g].start()
        for copy in writes:
            copy.wait()

    return pl.pallas_call(
        body,
        grid_spec=pltpu.PrefetchScalarGridSpec(
            num_scalar_prefetch=1,
            grid=(1,),
            in_specs=[pl.BlockSpec(memory_space=pl.ANY)] * len(chunks),
            out_specs=pl.BlockSpec(memory_space=pl.ANY),
            scratch_shapes=[pltpu.VMEM((groups, devices, count, 16, COLS), BF16) for count in counts]
            + [
                pltpu.VMEM((9 * PITCH, COLS), F32),
                pltpu.VMEM((groups, 8, WAVES, COLS), BF16),
                pltpu.SemaphoreType.DMA((groups, len(chunks))),
                pltpu.SemaphoreType.DMA((groups,)),
            ],
        ),
        out_shape=jax.ShapeDtypeStruct((rows, WAVES, COLS), BF16),
        compiler_params=pltpu.CompilerParams(vmem_limit_bytes=VMEM),
        cost_estimate=pl.CostEstimate(flops=0, bytes_accessed=26_000_000, transcendentals=0),
        name="scatter_waves",
    )(pair_table, *chunks)


def transform(orders, arrived, legendre, fold, unfold, weight, first_map, second_map, depth, damping, first):
    devices, count, groups = arrived.shape[:3]
    all_rows = devices * groups * 8

    def body(
        orders_ref, arrived_ref, legendre_ref, fold_ref, unfold_ref, weight_ref, map1_ref, map2_ref, depth_ref,
        damping_ref, out_ref, low_ref, high_ref, rows_in, folded, blocks, halves, tail,
    ):
        step = pl.program_id(0)
        order = orders_ref[first + step]

        @pl.when(step == 0)
        def _():
            low_ref[...] = jnp.zeros_like(low_ref)
            high_ref[...] = jnp.zeros_like(high_ref)
            tail[...] = jnp.zeros_like(tail)

        tail[0:1, :] = legendre_ref[0, NPACK - 1 : NPACK, :]

        arrived_rows = arrived_ref[...].astype(F32).reshape(devices * groups, 16, COLS)
        rows_in[:, :COLS] = arrived_rows[:, :8].reshape(all_rows, COLS).astype(BF16)
        rows_in[:, COLS:] = arrived_rows[:, 8:].reshape(all_rows, COLS).astype(BF16)

        def fold_tile(i, carry):
            at = pl.multiple_of(i * 128, 128)
            for part in range(2):
                sums = jnp.dot(
                    fold_ref[pl.ds(pl.multiple_of(part * NHALF + at, 128), 128), :],
                    rows_in[...],
                    preferred_element_type=F32,
                )
                folded[pl.ds(at, 128), part * 256 : part * 256 + 256] = (
                    weight_ref[pl.ds(at, 128), :] * sums
                ).astype(BF16)
            return carry

        lax.fori_loop(0, NHALF // 128, fold_tile, 0)

        def update(start, slab, size):
            gathered = jnp.dot(slab, folded[...], preferred_element_type=F32)
            packed = lax.broadcasted_iota(jnp.int32, (size, COLS), 0) + start
            in_first = packed <= TRUNC - order
            odd = jnp.where(in_first, packed, packed + order) % 2 == 1
            spectral = jnp.where(
                in_first,
                jnp.where(odd, gathered[:, 2 * COLS : 3 * COLS], gathered[:, :COLS]),
                jnp.where(odd, gathered[:, 3 * COLS :], gathered[:, COLS : 2 * COLS]),
            )
            degree = jnp.where(in_first, order + packed, packed - 1)
            scale = (degree * (degree + 1)).astype(F32) / F32(TRUNC * (TRUNC + 1))
            forced = jnp.dot(
                spectral, map1_ref[...], precision=lax.Precision.HIGHEST, preferred_element_type=F32
            )
            modal = (forced[:, :COLS] + scale * forced[:, COLS:]) / (1.0 + scale * depth_ref[...])
            evolved = jnp.dot(
                modal, map2_ref[...], precision=lax.Precision.HIGHEST, preferred_element_type=F32
            )
            field = (lax.broadcasted_iota(jnp.int32, (size, COLS), 1) // LEVELS) % FIELDS
            updated = (jnp.where(field == 1, 0.0, spectral) + evolved) / (
                1.0 + damping_ref[...] * (scale * scale)
            )
            energy = jnp.where(in_first & (order == 0), 1.0, 2.0) * (updated * updated)
            nothing = jnp.zeros_like(updated)
            for block, chosen in enumerate(
                (in_first & ~odd, ~in_first & ~odd, in_first & odd, ~in_first & odd)
            ):
                blocks[pl.ds(start, size), block * COLS : (block + 1) * COLS] = jnp.where(
                    chosen, updated, nothing
                ).astype(BF16)
            low = jnp.where(in_first, energy, nothing)
            high_ref[pl.ds(start, size), :] += energy - low
            return low

        def update_tile(i, carry):
            start = pl.multiple_of(i * KTILE, KTILE)
            low = update(start, legendre_ref[0, pl.ds(start, KTILE), :], KTILE)
            low_ref[pl.ds(start + order, KTILE), :] += low
            return carry

        lax.fori_loop(0, (NPACK - 1) // KTILE, update_tile, 0)
        update(NPACK - 1, tail[...], NTAIL)

        def synthesis_tile(i, carry):
            at = pl.multiple_of(i * 128, 128)
            both = lax.dot_general(
                legendre_ref[0, : NPACK - 1, pl.ds(at, 128)],
                blocks[: NPACK - 1, :],
                (((0,), (0,)), ((), ())),
                preferred_element_type=F32,
            ) + lax.dot_general(
                tail[:, pl.ds(at, 128)],
                blocks[NPACK - 1 :, :],
                (((0,), (0,)), ((), ())),
                preferred_element_type=F32,
            )
            halves[pl.ds(at, 128), :] = (both[:, :256] + both[:, 256:]).astype(BF16)
            halves[pl.ds(pl.multiple_of(NHALF + at, 128), 128), :] = (
                both[:, :256] - both[:, 256:]
            ).astype(BF16)
            return carry

        lax.fori_loop(0, NHALF // 128, synthesis_tile, 0)

        back = jnp.dot(unfold_ref[...], halves[...], preferred_element_type=F32)
        both = jnp.concatenate(
            [
                back[:, :COLS].reshape(devices * groups, 8, COLS),
                back[:, COLS:].reshape(devices * groups, 8, COLS),
            ],
            axis=1,
        )
        out_ref[...] = both.astype(BF16).reshape(devices, 1, groups, 16, COLS)

    whole = lambda shape: pl.BlockSpec(shape, lambda i, t: (0,) * len(shape))
    return pl.pallas_call(
        body,
        grid_spec=pltpu.PrefetchScalarGridSpec(
            num_scalar_prefetch=1,
            grid=(count,),
            in_specs=[
                pl.BlockSpec((devices, 1, groups, 16, COLS), lambda i, t: (0, i, 0, 0, 0)),
                pl.BlockSpec((1, NPACK, NHALF), lambda i, t: (first + i, 0, 0)),
                whole(fold.shape),
                whole(unfold.shape),
                whole(weight.shape),
                whole(first_map.shape),
                whole(second_map.shape),
                whole(depth.shape),
                whole(damping.shape),
            ],
            out_specs=[
                pl.BlockSpec((devices, 1, groups, 16, COLS), lambda i, t: (0, i, 0, 0, 0)),
                whole((2 * WAVES, COLS)),
                whole((WAVES + NTAIL, COLS)),
            ],
            scratch_shapes=[
                pltpu.VMEM((all_rows, 2 * COLS), BF16),
                pltpu.VMEM((NHALF, 4 * COLS), BF16),
                pltpu.VMEM((WAVES + NTAIL, 4 * COLS), BF16),
                pltpu.VMEM((NLAT, 2 * COLS), BF16),
                pltpu.VMEM((NTAIL, NHALF), BF16),
            ],
        ),
        out_shape=[
            jax.ShapeDtypeStruct(arrived.shape, BF16),
            jax.ShapeDtypeStruct((2 * WAVES, COLS), F32),
            jax.ShapeDtypeStruct((WAVES + NTAIL, COLS), F32),
        ],
        compiler_params=pltpu.CompilerParams(vmem_limit_bytes=VMEM),
        cost_estimate=pl.CostEstimate(
            flops=count * 3_500_000_000, bytes_accessed=count * 3_000_000, transcendentals=0
        ),
        name="transform",
    )(orders, arrived, legendre, fold, unfold, weight, first_map, second_map, depth, damping)


def field_map(parts):
    one = jnp.zeros((FIELDS, LEVELS, FIELDS, LEVELS), F32)
    for source, target, matrix in parts:
        one = one.at[source, :, target, :].set(matrix)
    one = one.reshape(COLS // 2, COLS // 2)
    nothing = jnp.zeros_like(one)
    return jnp.concatenate(
        [jnp.concatenate([one, nothing], axis=1), jnp.concatenate([nothing, one], axis=1)], axis=0
    )


def scatter_sum(parts, devices):
    device = lax.axis_index(AXES)
    sums = parts.reshape(devices, -1, COLS)
    bit = 1
    while bit < devices:
        sums = sums.reshape((sums.shape[0] // 2, 2) + sums.shape[1:])
        own = (device // bit) % 2
        kept = lax.dynamic_index_in_dim(sums, own, 1, keepdims=False)
        sent = lax.dynamic_index_in_dim(sums, 1 - own, 1, keepdims=False)
        came = lax.ppermute(sent, AXES, [(d, d ^ bit) for d in range(devices)])
        sums = kept + came
        bit *= 2
    return kept, came


def exchange(block):
    flat = block.reshape(block.shape[0], -1, COLS)
    return lax.all_to_all(flat, AXES, 0, 0, tiled=True).reshape(block.shape)


def on_device(
    fourier, legendre, pair_table, row_lat, gauss_weight, layer_pressure_matrix, modes, mode_depth, diffusion
):
    devices = lax.axis_size("lat") * lax.axis_size("wave")
    rows = fourier.shape[0]
    local_pairs = legendre.shape[0]
    padded = -(-rows // 8) * 8
    chunks = min(2, local_pairs)
    cuts = [local_pairs * c // chunks for c in range(chunks + 1)]
    spans = [(cuts[c], cuts[c + 1] - cuts[c]) for c in range(chunks)]
    own = lax.dynamic_slice_in_dim(
        pair_table, lax.axis_index(AXES) * local_pairs, local_pairs
    )

    lat = jnp.pad(
        row_lat.reshape(devices, rows), ((0, 0), (0, padded - rows)), constant_values=-1
    ).reshape(-1)
    half = jnp.arange(NHALF, dtype=jnp.int32)
    north_rows = (lat[None, :] == half[:, None]).astype(BF16)
    south_rows = (lat[None, :] == NLAT - 1 - half[:, None]).astype(BF16)
    fold = jnp.concatenate([north_rows + south_rows, north_rows - south_rows], axis=0)
    unfold = jnp.concatenate(
        [lat[:, None] == half[None, :], lat[:, None] == NLAT - 1 - half[None, :]], axis=1
    ).astype(BF16)
    high = lax.Precision.HIGHEST
    first_map = jnp.concatenate(
        [
            field_map([(1, 1, modes)]),
            field_map([(2, 1, jnp.dot(layer_pressure_matrix, modes, precision=high))]),
        ],
        axis=1,
    )
    second_map = field_map(
        [
            (1, 1, modes.T),
            (1, 2, -jnp.dot(modes.T, layer_pressure_matrix.T, precision=high)),
        ]
    )
    depth = jnp.tile(
        jnp.zeros((FIELDS, LEVELS), F32).at[1].set(mode_depth).reshape(1, -1), (1, 2)
    )
    damping = jnp.tile(diffusion.reshape(1, -1), (1, 2))

    outgoing = [
        gather_waves(pair_table, fourier, devices, local_pairs, first, count)
        for first, count in spans
    ]
    arrived = [exchange(block) for block in outgoing]
    done = [
        transform(
            own, block, legendre, fold, unfold, gauss_weight.reshape(NHALF, 1), first_map, second_map,
            depth, damping, first,
        )
        for block, (first, _) in zip(arrived, spans)
    ]
    energy = sum(low[:WAVES] + high[1 : WAVES + 1] for _, low, high in done)
    halves = scatter_sum(energy[:, : COLS // 2] + energy[:, COLS // 2 :], devices)
    back = [exchange(block) for block, _, _ in done]
    fourier_out = scatter_waves(pair_table, back, rows, local_pairs)
    fourier_out, *halves = lax.optimization_barrier((fourier_out, *halves))
    spectrum = (halves[0] + halves[1]).reshape(NLAT // devices, FIELDS * LEVELS)
    return (fourier_out, spectrum)


def solution(mesh):
    split = P(AXES, None, None)
    placed = (split, split, P(), P(), P(), P(), P(), P(), P())
    return jax.shard_map(
        on_device,
        mesh=mesh,
        in_specs=placed,
        out_specs=(split, P(AXES, None)),
        check_vma=False,
    )
```

```python
import jax
import jax.numpy as jnp
from jax import lax
from jax.experimental import pallas as pl
from jax.experimental.pallas import tpu as pltpu
from jax.sharding import PartitionSpec as P

TRUNC = 1279
NLAT = 1280
FIELDS = 4
LEVELS = 16
WAVES = 1280
NPACK = 1281
NHALF = 640
COLS = 128
PITCH = 1288
KTILE = 256
NTAIL = 16
AXES = ("lat", "wave")
VMEM = 60 << 20
BF16 = jnp.bfloat16
F32 = jnp.float32


def divisor_up_to(number, most):
    return max(d for d in range(1, most + 1) if number % d == 0)


def row_groups(rows):
    return [(at, min(8, rows - at)) for at in range(0, rows, 8)]


def gather_waves(pair_table, fourier, devices, local_pairs, first, count):
    rows = fourier.shape[0]
    spans = row_groups(rows)
    groups = len(spans)

    def body(table, rows_ref, out_ref, read, held, written, read_sem, write_sem):
        reads = [
            pltpu.make_async_copy(rows_ref.at[pl.ds(at, size)], read.at[pl.ds(at, size)], read_sem.at[g])
            for g, (at, size) in enumerate(spans)
        ]
        writes = [
            pltpu.make_async_copy(written.at[g], out_ref.at[:, :, g], write_sem.at[g])
            for g in range(groups)
        ]
        for copy in reads:
            copy.start()
        if rows % 8:
            read[rows:] = jnp.zeros((groups * 8 - rows, WAVES, COLS), BF16)

        for g in range(groups):
            reads[g].wait()

            def widen(r, carry, g=g):
                held[pl.ds(pl.multiple_of(r * PITCH, 8), WAVES), :] = read[g * 8 + r].astype(F32)
                return carry

            lax.fori_loop(0, 8, widen, 0)

            def one_device(d, carry, g=g):
                for s in range(count):
                    wave = table[d * local_pairs + first + s]
                    both = jnp.concatenate(
                        [
                            held[pl.ds(wave, 8, stride=PITCH), :],
                            held[pl.ds(TRUNC - wave, 8, stride=PITCH), :],
                        ],
                        axis=0,
                    )
                    written[g, d, s] = both.astype(BF16)
                return carry

            lax.fori_loop(0, devices, one_device, 0)
            writes[g].start()
        for copy in writes:
            copy.wait()

    return pl.pallas_call(
        body,
        grid_spec=pltpu.PrefetchScalarGridSpec(
            num_scalar_prefetch=1,
            grid=(1,),
            in_specs=[pl.BlockSpec(memory_space=pl.ANY)],
            out_specs=pl.BlockSpec(memory_space=pl.ANY),
            scratch_shapes=[
                pltpu.VMEM((groups * 8, WAVES, COLS), BF16),
                pltpu.VMEM((9 * PITCH, COLS), F32),
                pltpu.VMEM((groups, devices, count, 16, COLS), BF16),
                pltpu.SemaphoreType.DMA((groups,)),
                pltpu.SemaphoreType.DMA((groups,)),
            ],
        ),
        out_shape=jax.ShapeDtypeStruct((devices, count, groups, 16, COLS), BF16),
        compiler_params=pltpu.CompilerParams(vmem_limit_bytes=VMEM),
        cost_estimate=pl.CostEstimate(flops=0, bytes_accessed=20_000_000, transcendentals=0),
        name="gather_waves",
    )(pair_table, fourier)


def scatter_waves(pair_table, chunks, rows, local_pairs):
    devices = chunks[0].shape[0]
    spans = row_groups(rows)
    groups = len(spans)
    counts = [chunk.shape[1] for chunk in chunks]

    def body(table, *refs):
        chunk_refs = refs[: len(chunks)]
        out_ref = refs[len(chunks)]
        parts = refs[len(chunks) + 1 : 2 * len(chunks) + 1]
        held, written, read_sem, write_sem = refs[2 * len(chunks) + 1 :]
        reads = [
            [
                pltpu.make_async_copy(chunk.at[:, :, g], part.at[g], read_sem.at[g, c])
                for c, (chunk, part) in enumerate(zip(chunk_refs, parts))
            ]
            for g in range(groups)
        ]
        writes = [
            pltpu.make_async_copy(
                written.at[g, pl.ds(0, size)], out_ref.at[pl.ds(at, size)], write_sem.at[g]
            )
            for g, (at, size) in enumerate(spans)
        ]
        for group in reads:
            for copy in group:
                copy.start()

        for g in range(groups):
            for copy in reads[g]:
                copy.wait()

            def one_device(d, carry, g=g):
                slot = 0
                for part, count in zip(parts, counts):
                    for s in range(count):
                        wave = table[d * local_pairs + slot]
                        both = part[g, d, s].astype(F32)
                        held[pl.ds(wave, 8, stride=PITCH), :] = both[:8]
                        held[pl.ds(TRUNC - wave, 8, stride=PITCH), :] = both[8:]
                        slot += 1
                return carry

            lax.fori_loop(0, devices, one_device, 0)

            def narrow(r, carry, g=g):
                row = held[pl.ds(pl.multiple_of(r * PITCH, 8), WAVES), :]
                written[g, r] = row.astype(BF16)
                return carry

            lax.fori_loop(0, 8, narrow, 0)
            writes[g].start()
        for copy in writes:
            copy.wait()

    return pl.pallas_call(
        body,
        grid_spec=pltpu.PrefetchScalarGridSpec(
            num_scalar_prefetch=1,
            grid=(1,),
            in_specs=[pl.BlockSpec(memory_space=pl.ANY)] * len(chunks),
            out_specs=pl.BlockSpec(memory_space=pl.ANY),
            scratch_shapes=[pltpu.VMEM((groups, devices, count, 16, COLS), BF16) for count in counts]
            + [
                pltpu.VMEM((9 * PITCH, COLS), F32),
                pltpu.VMEM((groups, 8, WAVES, COLS), BF16),
                pltpu.SemaphoreType.DMA((groups, len(chunks))),
                pltpu.SemaphoreType.DMA((groups,)),
            ],
        ),
        out_shape=jax.ShapeDtypeStruct((rows, WAVES, COLS), BF16),
        compiler_params=pltpu.CompilerParams(vmem_limit_bytes=VMEM),
        cost_estimate=pl.CostEstimate(flops=0, bytes_accessed=26_000_000, transcendentals=0),
        name="scatter_waves",
    )(pair_table, *chunks)


def transform(orders, arrived, legendre, fold, unfold, weight, first_map, second_map, depth, damping, first):
    devices, count, groups = arrived.shape[:3]
    all_rows = devices * groups * 8

    def body(
        orders_ref, arrived_ref, legendre_ref, fold_ref, unfold_ref, weight_ref, map1_ref, map2_ref, depth_ref,
        damping_ref, out_ref, low_ref, high_ref, rows_in, folded, analysed, blocks, halves, tail,
    ):
        step = pl.program_id(0)
        order = orders_ref[first + step]

        @pl.when(step == 0)
        def _():
            low_ref[...] = jnp.zeros_like(low_ref)
            high_ref[...] = jnp.zeros_like(high_ref)
            tail[...] = jnp.zeros_like(tail)

        tail[0:1, :] = legendre_ref[0, NPACK - 1 : NPACK, :]

        arrived_rows = arrived_ref[...].astype(F32).reshape(devices * groups, 16, COLS)
        rows_in[:, :COLS] = arrived_rows[:, :8].reshape(all_rows, COLS).astype(BF16)
        rows_in[:, COLS:] = arrived_rows[:, 8:].reshape(all_rows, COLS).astype(BF16)

        folds = weight_ref[...] * jnp.dot(fold_ref[...], rows_in[...], preferred_element_type=F32)
        folded[:, :256] = folds[:NHALF].astype(BF16)
        folded[:, 256:] = folds[NHALF:].astype(BF16)
        analysed[: NPACK - 1, :] = jnp.dot(
            legendre_ref[0, : NPACK - 1, :], folded[...], preferred_element_type=F32
        )
        analysed[NPACK - 1 :, :] = jnp.dot(tail[...], folded[...], preferred_element_type=F32)

        def update(start, size):
            gathered = analysed[pl.ds(start, size), :]
            packed = lax.broadcasted_iota(jnp.int32, (size, COLS), 0) + start
            in_first = packed <= TRUNC - order
            odd = jnp.where(in_first, packed, packed + order) % 2 == 1
            spectral = jnp.where(
                in_first,
                jnp.where(odd, gathered[:, 2 * COLS : 3 * COLS], gathered[:, :COLS]),
                jnp.where(odd, gathered[:, 3 * COLS :], gathered[:, COLS : 2 * COLS]),
            )
            degree = jnp.where(in_first, order + packed, packed - 1)
            scale = (degree * (degree + 1)).astype(F32) / F32(TRUNC * (TRUNC + 1))
            forced = jnp.dot(
                spectral, map1_ref[...], precision=lax.Precision.HIGHEST, preferred_element_type=F32
            )
            modal = (forced[:, :COLS] + scale * forced[:, COLS:]) / (1.0 + scale * depth_ref[...])
            evolved = jnp.dot(
                modal, map2_ref[...], precision=lax.Precision.HIGHEST, preferred_element_type=F32
            )
            field = (lax.broadcasted_iota(jnp.int32, (size, COLS), 1) // LEVELS) % FIELDS
            updated = (jnp.where(field == 1, 0.0, spectral) + evolved) / (
                1.0 + damping_ref[...] * (scale * scale)
            )
            energy = jnp.where(in_first & (order == 0), 1.0, 2.0) * (updated * updated)
            nothing = jnp.zeros_like(updated)
            for block, chosen in enumerate(
                (in_first & ~odd, ~in_first & ~odd, in_first & odd, ~in_first & odd)
            ):
                blocks[pl.ds(start, size), block * COLS : (block + 1) * COLS] = jnp.where(
                    chosen, updated, nothing
                ).astype(BF16)
            low = jnp.where(in_first, energy, nothing)
            high_ref[pl.ds(start, size), :] += energy - low
            return low

        def update_tile(i, carry):
            start = pl.multiple_of(i * KTILE, KTILE)
            low = update(start, KTILE)
            low_ref[pl.ds(start + order, KTILE), :] += low
            return carry

        lax.fori_loop(0, (NPACK - 1) // KTILE, update_tile, 0)
        update(NPACK - 1, NTAIL)

        synthesised = lax.dot_general(
            legendre_ref[0, : NPACK - 1, :],
            blocks[: NPACK - 1, :],
            (((0,), (0,)), ((), ())),
            preferred_element_type=F32,
        ) + lax.dot_general(
            tail[...], blocks[NPACK - 1 :, :], (((0,), (0,)), ((), ())), preferred_element_type=F32
        )
        halves[:NHALF, :] = (synthesised[:, :256] + synthesised[:, 256:]).astype(BF16)
        halves[NHALF:, :] = (synthesised[:, :256] - synthesised[:, 256:]).astype(BF16)

        back = jnp.dot(unfold_ref[...], halves[...], preferred_element_type=F32)
        both = jnp.concatenate(
            [
                back[:, :COLS].reshape(devices * groups, 8, COLS),
                back[:, COLS:].reshape(devices * groups, 8, COLS),
            ],
            axis=1,
        )
        out_ref[...] = both.astype(BF16).reshape(devices, 1, groups, 16, COLS)

    whole = lambda shape: pl.BlockSpec(shape, lambda i, t: (0,) * len(shape))
    return pl.pallas_call(
        body,
        grid_spec=pltpu.PrefetchScalarGridSpec(
            num_scalar_prefetch=1,
            grid=(count,),
            in_specs=[
                pl.BlockSpec((devices, 1, groups, 16, COLS), lambda i, t: (0, i, 0, 0, 0)),
                pl.BlockSpec((1, NPACK, NHALF), lambda i, t: (first + i, 0, 0)),
                whole(fold.shape),
                whole(unfold.shape),
                whole(weight.shape),
                whole(first_map.shape),
                whole(second_map.shape),
                whole(depth.shape),
                whole(damping.shape),
            ],
            out_specs=[
                pl.BlockSpec((devices, 1, groups, 16, COLS), lambda i, t: (0, i, 0, 0, 0)),
                whole((2 * WAVES, COLS)),
                whole((WAVES + NTAIL, COLS)),
            ],
            scratch_shapes=[
                pltpu.VMEM((all_rows, 2 * COLS), BF16),
                pltpu.VMEM((NHALF, 4 * COLS), BF16),
                pltpu.VMEM((WAVES + NTAIL, 4 * COLS), F32),
                pltpu.VMEM((WAVES + NTAIL, 4 * COLS), BF16),
                pltpu.VMEM((NLAT, 2 * COLS), BF16),
                pltpu.VMEM((NTAIL, NHALF), BF16),
            ],
        ),
        out_shape=[
            jax.ShapeDtypeStruct(arrived.shape, BF16),
            jax.ShapeDtypeStruct((2 * WAVES, COLS), F32),
            jax.ShapeDtypeStruct((WAVES + NTAIL, COLS), F32),
        ],
        compiler_params=pltpu.CompilerParams(vmem_limit_bytes=VMEM),
        cost_estimate=pl.CostEstimate(
            flops=count * 3_500_000_000, bytes_accessed=count * 3_000_000, transcendentals=0
        ),
        name="transform",
    )(orders, arrived, legendre, fold, unfold, weight, first_map, second_map, depth, damping)


def field_map(parts):
    one = jnp.zeros((FIELDS, LEVELS, FIELDS, LEVELS), F32)
    for source, target, matrix in parts:
        one = one.at[source, :, target, :].set(matrix)
    one = one.reshape(COLS // 2, COLS // 2)
    nothing = jnp.zeros_like(one)
    return jnp.concatenate(
        [jnp.concatenate([one, nothing], axis=1), jnp.concatenate([nothing, one], axis=1)], axis=0
    )


def scatter_sum(parts, devices):
    device = lax.axis_index(AXES)
    sums = parts.reshape(devices, -1, COLS)
    bit = 1
    while bit < devices:
        sums = sums.reshape((sums.shape[0] // 2, 2) + sums.shape[1:])
        own = (device // bit) % 2
        kept = lax.dynamic_index_in_dim(sums, own, 1, keepdims=False)
        sent = lax.dynamic_index_in_dim(sums, 1 - own, 1, keepdims=False)
        came = lax.ppermute(sent, AXES, [(d, d ^ bit) for d in range(devices)])
        sums = kept + came
        bit *= 2
    return kept, came


def exchange(block):
    flat = block.reshape(block.shape[0], -1, COLS)
    return lax.all_to_all(flat, AXES, 0, 0, tiled=True).reshape(block.shape)


def on_device(
    fourier, legendre, pair_table, row_lat, gauss_weight, layer_pressure_matrix, modes, mode_depth, diffusion
):
    devices = lax.axis_size("lat") * lax.axis_size("wave")
    rows = fourier.shape[0]
    local_pairs = legendre.shape[0]
    padded = -(-rows // 8) * 8
    chunks = min(2, local_pairs)
    cuts = [0, -(-local_pairs * 9 // 20), local_pairs][: chunks + 1]
    spans = [(cuts[c], cuts[c + 1] - cuts[c]) for c in range(chunks)]
    own = lax.dynamic_slice_in_dim(
        pair_table, lax.axis_index(AXES) * local_pairs, local_pairs
    )

    lat = jnp.pad(
        row_lat.reshape(devices, rows), ((0, 0), (0, padded - rows)), constant_values=-1
    ).reshape(-1)
    half = jnp.arange(NHALF, dtype=jnp.int32)
    north_rows = (lat[None, :] == half[:, None]).astype(BF16)
    south_rows = (lat[None, :] == NLAT - 1 - half[:, None]).astype(BF16)
    fold = jnp.concatenate([north_rows + south_rows, north_rows - south_rows], axis=0)
    unfold = jnp.concatenate(
        [lat[:, None] == half[None, :], lat[:, None] == NLAT - 1 - half[None, :]], axis=1
    ).astype(BF16)
    high = lax.Precision.HIGHEST
    first_map = jnp.concatenate(
        [
            field_map([(1, 1, modes)]),
            field_map([(2, 1, jnp.dot(layer_pressure_matrix, modes, precision=high))]),
        ],
        axis=1,
    )
    second_map = field_map(
        [
            (1, 1, modes.T),
            (1, 2, -jnp.dot(modes.T, layer_pressure_matrix.T, precision=high)),
        ]
    )
    depth = jnp.tile(
        jnp.zeros((FIELDS, LEVELS), F32).at[1].set(mode_depth).reshape(1, -1), (1, 2)
    )
    damping = jnp.tile(diffusion.reshape(1, -1), (1, 2))

    outgoing = [
        gather_waves(pair_table, fourier, devices, local_pairs, first, count)
        for first, count in spans
    ]
    arrived = [exchange(block) for block in outgoing]
    done = [
        transform(
            own, block, legendre, fold, unfold, jnp.tile(gauss_weight, 2).reshape(2 * NHALF, 1), first_map, second_map,
            depth, damping, first,
        )
        for block, (first, _) in zip(arrived, spans)
    ]
    energy = sum(low[:WAVES] + high[1 : WAVES + 1] for _, low, high in done)
    halves = scatter_sum(energy[:, : COLS // 2] + energy[:, COLS // 2 :], devices)
    back = [exchange(block) for block, _, _ in done]
    fourier_out = scatter_waves(pair_table, back, rows, local_pairs)
    fourier_out, *halves = lax.optimization_barrier((fourier_out, *halves))
    spectrum = (halves[0] + halves[1]).reshape(NLAT // devices, FIELDS * LEVELS)
    return (fourier_out, spectrum)


def solution(mesh):
    split = P(AXES, None, None)
    placed = (split, split, P(), P(), P(), P(), P(), P(), P())
    return jax.shard_map(
        on_device,
        mesh=mesh,
        in_specs=placed,
        out_specs=(split, P(AXES, None)),
        check_vma=False,
    )
```
